32 devices in a mesh: dp: 4 (over y, x), mx: 4 (over z), my: 2 (over core).
Axes of the slice: x: 2, y: 2, z: 4, core: 2. Of those that a mesh axis runs over, the one named last changes fastest.
Arguments:
- block_entry_rows: bfloat16 [8192, 768], P(('dp', 'my'), 'mx'), may hold values from -6 to 6
- cotangent: bfloat16 [8192, 768], P(('dp', 'my'), 'mx'), may hold values from -6 to 6
- gain_one: float32 [768], replicated, may hold values from 0.5 to 1.5
- w_qkv: bfloat16 [768, 3, 768], P('my', None, 'mx'), may hold values from -0.21875 to 0.21875
- w_out_attn: bfloat16 [768, 768], P('mx', 'my'), may hold values from -3.5 to 3.5
- rel_bias: float32 [12, 32], replicated, may hold values from -4 to 4
- gain_two: float32 [768], replicated, may hold values from 0.5 to 1.5
- router: bfloat16 [768, 8], replicated, may hold values from -0.21875 to 0.21875
- w_in: bfloat16 [8, 768, 3072], P('dp', 'my', 'mx'), may hold values from -0.21875 to 0.21875
- w_out: bfloat16 [8, 3072, 768], P('dp', 'mx', 'my'), may hold values from -0.109375 to 0.109375
- routes: int32 [8192, 2], P(('dp', 'my')), may hold values from 0 to 7, all different within a row
- slot_order: int32 [8, 2048], P(('dp', 'my')), may hold values from 0 to 2047, each once within a row
- cont_ids: int32 [4, 1024], P('dp'), may hold values from 0 to 7, never falling along the last dimension, each value on 1 to 256 neighbouring positions
Outputs:
- block_output: float32 [8192, 768], P(('dp', 'my'), 'mx')
- d_x: float32 [8192, 768], P(('dp', 'my'), 'mx')
- d_w_qkv: float32 [768, 3, 768], P('my', None, 'mx')
- d_w_out_attn: float32 [768, 768], P('mx', 'my')
- d_rel_bias: float32 [12, 32], replicated
- d_gain_one: float32 [768], replicated
- d_gain_two: float32 [768], replicated
- d_router: float32 [768, 8], replicated
- d_w_in: float32 [8, 768, 3072], P('dp', 'my', 'mx')
- d_w_out: float32 [8, 3072, 768], P('dp', 'mx', 'my')
The draws below stay inside these ranges and needn't reach their ends.
Inputs may be any that keep to these rules, and one draw needn't show every extreme that they name: `routes`: each token names two different experts. `slot_order`: each row is an ordering of 0 to 2047, each number once. `cont_ids`: never falling along a row; every continuation has 1 to 256 tokens, and one has exactly 256.
All inputs are finite; a program needn't handle non-finite values.
Results may differ from the reference program's by a relative error of at most 0.022.
Values may be sent and summed in bfloat16 or wider, within the bound.
No kernel may reach another device: no remote copies, remote signals or barrier semaphores. Data moves between devices by JAX's collectives and lax.ppermute only.
A program may use at most 256 MiB of HBM per device.

```python
import math
import jax
import jax.numpy as jnp
import numpy as np
from jax import lax

MODEL_WIDTH = 768
HEADS = 12
HEAD = 64
FF = 3072
TOK_DEV = 1024
SEGS = 8
NB = 32
EXPERTS = 8
CAP = 256
BUCKET = 32
TOKENS = 8192
N_DP = 4


def levels(rng, dims, pieces, smallest, largest):
    loudness = 1.0
    for dim, parts in pieces:
        draws = jax.random.uniform(jax.random.fold_in(jax.random.fold_in(rng, 6), dim), (parts,), jnp.float32, smallest / len(pieces), largest / len(pieces))
        loudness = loudness * jnp.repeat(jnp.exp(draws), dims[dim] // parts).reshape((-1,) + (1,) * (len(dims) - 1 - dim))
    return loudness


def choose_distinct(key, rows, amount, top, lift):
    sequence = jax.random.permutation(jax.random.fold_in(key, 1), amount)
    boost = sequence
    for power in range(3):
        boost = boost * boost // amount
    boost = boost * lift // amount
    lots = jax.random.randint(jax.random.fold_in(key, 2), (rows, amount), 0, 4096) + boost
    sure = jax.random.permutation(jax.random.fold_in(key, 3), rows)[jnp.arange(amount) % rows]
    lots = jnp.where(jnp.arange(rows)[:, None] == sure[None, :], 1 << 14, lots)
    priority = lots * amount + jnp.arange(amount)
    return lax.top_k(priority.astype(jnp.int32), top)[1].astype(jnp.int32)


def profile(count, total, most, skew):
    weights = [(1 << 20) // math.isqrt(rank ** skew) + 1 for rank in range(2, count + 1)]
    rest, counts = total - most - (count - 1), [1] * (count - 1)
    while rest > 0:
        free = [i for i in range(count - 1) if counts[i] < most]
        whole, left = sum([weights[i] for i in free]), rest
        for i in free:
            extra = min(most - counts[i], max(1, left * weights[i] // whole), rest)
            counts[i] = counts[i] + extra
            rest = rest - extra
    return np.array([most] + counts)


def uneven(rng, number_of, total, reach, slope):
    if number_of == 2:
        one = jax.random.randint(rng, (), max(1, total - reach), min(reach, total - 1) + 1)
        return jnp.stack([one, total - one])
    tallies = jnp.asarray(profile(number_of, total, reach, slope), jnp.int32)
    couples = (number_of - 1) // 2
    donor, receiver = tallies[1:1 + 2 * couples:2], tallies[2:2 + 2 * couples:2]
    room = jnp.minimum(donor - 1, reach - receiver)
    shifted = jax.random.randint(jax.random.fold_in(rng, 1), (couples,), 0, 1 << 20) % (room + 1)
    tallies = tallies.at[1:1 + 2 * couples:2].set(donor - shifted).at[2:2 + 2 * couples:2].set(receiver + shifted)
    return tallies[jax.random.permutation(jax.random.fold_in(rng, 2), number_of)]


def gaussian(stream_key, shape, deviation, reach, split=(), held_as=jnp.bfloat16):
    loudness = levels(stream_key, shape, split, -0.22, 0.18) if split else 1.0
    array = jax.random.normal(stream_key, shape, jnp.float32) * deviation * loudness
    return jnp.minimum(jnp.maximum(array, -reach), reach).astype(held_as)


def setup_inputs(seed: int = 0) -> dict:
    seeds = jax.random.split(jax.random.key(seed), 14)
    block_entry_rows = gaussian(seeds[0], (TOKENS, MODEL_WIDTH), 1.0, 6.0, ((0, 8), (1, 4)))
    cotangent = gaussian(seeds[1], (TOKENS, MODEL_WIDTH), 1.0, 6.0, ((0, 8), (1, 4)))
    gain_one = jnp.clip(1.0 + 0.1 * jax.random.normal(seeds[2], (MODEL_WIDTH,), jnp.float32), 0.5, 1.5)
    w_qkv = gaussian(seeds[3], (MODEL_WIDTH, 3, HEADS * HEAD), MODEL_WIDTH ** -0.5, 0.21875, ((0, 2), (2, 4)))
    w_out_attn = gaussian(seeds[4], (HEADS * HEAD, MODEL_WIDTH), (max(HEADS * HEAD // 256, 1)) ** -0.5, 3.5, ((0, 4), (1, 2)))
    rel_bias = gaussian(seeds[5], (HEADS, NB), 1.0, 4.0, (), jnp.float32)
    gain_two = jnp.clip(1.0 + 0.1 * jax.random.normal(seeds[6], (MODEL_WIDTH,), jnp.float32), 0.5, 1.5)
    router = gaussian(seeds[7], (MODEL_WIDTH, EXPERTS), MODEL_WIDTH ** -0.5, 0.21875)
    w_in = gaussian(seeds[8], (EXPERTS, MODEL_WIDTH, FF), MODEL_WIDTH ** -0.5, 0.21875, ((0, 4), (1, 2), (2, 4)))
    w_out = gaussian(seeds[9], (EXPERTS, FF, MODEL_WIDTH), FF ** -0.5, 0.109375, ((0, 4), (1, 4), (2, 2)))
    routes = choose_distinct(seeds[10], TOKENS, EXPERTS, 2, 2048)
    slot_order = jax.vmap(lambda own: jax.random.permutation(own, 2 * TOK_DEV))(jax.random.split(seeds[11], (2 * N_DP))).reshape((2 * N_DP, 2 * TOK_DEV)).astype(jnp.int32)
    cont_ids = jax.vmap(lambda own: jnp.searchsorted(jnp.cumsum(uneven(own, SEGS, TOK_DEV, TOK_DEV // 4, 1)), jnp.arange(TOK_DEV), side="right"))(jax.random.split(seeds[12], N_DP)).reshape((N_DP, TOK_DEV)).astype(jnp.int32)
    return {"block_entry_rows": block_entry_rows, "cotangent": cotangent, "gain_one": gain_one, "w_qkv": w_qkv, "w_out_attn": w_out_attn, "rel_bias": rel_bias, "gain_two": gain_two, "router": router, "w_in": w_in, "w_out": w_out, "routes": routes, "slot_order": slot_order, "cont_ids": cont_ids}


HIGH = lax.Precision.HIGHEST
EPS = 1e-06
NEG = -1e+30

@jax.custom_vjp
def low(v):
    return lax.optimization_barrier(v.astype(jnp.bfloat16)).astype(jnp.float32)

@jax.custom_vjp
def low_back(v):
    return v

def low_keep(v):
    return (low(v), None)

def low_pass(kept, grad):
    return (grad,)

def back_keep(v):
    return (v, None)

def back_low(kept, grad):
    return (low(grad),)
low.defvjp(low_keep, low_pass)
low_back.defvjp(back_keep, back_low)

def rms_norm(values, gain):
    return values * lax.rsqrt(lax.optimization_barrier(jnp.mean(values * values, axis=-1, keepdims=True)) + EPS) * gain

def slot_table(route_rows, order):
    flat = route_rows.reshape(-1)
    ranked = flat[order]
    one_hot = (ranked[:, None] == jnp.arange(EXPERTS, dtype=jnp.int32)[None, :]).astype(jnp.int32)
    before = jnp.cumsum(one_hot, axis=0) - one_hot
    rank_sorted = lax.optimization_barrier(jnp.sum(before * one_hot, axis=1))
    ranking = jnp.zeros_like(flat).at[order].set(rank_sorted)
    kept = ranking < CAP
    slot_id = flat * CAP + jnp.minimum(ranking, CAP - 1)
    target = jnp.where(kept, slot_id, EXPERTS * CAP)
    source = jnp.zeros((EXPERTS * CAP,), jnp.int32).at[target].set(jnp.arange(flat.shape[0], dtype=jnp.int32), mode='drop')
    filled = jnp.zeros((EXPERTS * CAP,), jnp.int32).at[target].set(1, mode='drop')
    return (slot_id, kept, source, filled)

def attend_group(group_in, gain_one, w_qkv, w_out_attn, rel_bias):
    x_group, seg_ids = group_in
    index = jnp.arange(TOK_DEV, dtype=jnp.int32)
    same_seg = seg_ids[:, None] == seg_ids[None, :]
    first_pos = lax.optimization_barrier(jnp.min(jnp.where(same_seg, index[None, :], TOK_DEV), axis=1))
    position = jnp.concatenate([index, TOK_DEV + index - first_pos])
    seg_full = jnp.concatenate([jnp.full((TOK_DEV,), -1, jnp.int32), seg_ids])
    every = jnp.arange(2 * TOK_DEV, dtype=jnp.int32)
    allowed = (every[None, :] <= every[:, None]) & ((every[None, :] < TOK_DEV) | (seg_full[None, :] == seg_full[:, None]))
    distance = jnp.maximum(position[:, None] - position[None, :], 0)
    bucket = jnp.minimum(distance // BUCKET, NB - 1)
    inner = HEADS * HEAD
    normed = low(rms_norm(x_group, gain_one))
    projected = low_back(low(jnp.dot(normed, w_qkv.reshape(MODEL_WIDTH, 3 * inner), precision=HIGH)))
    queries = projected[:, :inner].reshape(2 * TOK_DEV, HEADS, HEAD)
    keys_all = projected[:, inner:2 * inner].reshape(2 * TOK_DEV, HEADS, HEAD)
    values_all = projected[:, 2 * inner:].reshape(2 * TOK_DEV, HEADS, HEAD)
    scores = jnp.einsum('qhd,khd->hqk', queries, keys_all, precision=HIGH) * HEAD ** (-0.5) + rel_bias[:, bucket]
    scores = jnp.where(allowed[None], low_back(scores), NEG)
    probs = jax.nn.softmax(scores, axis=-1)
    mixed = jnp.einsum('hqk,khd->qhd', low(probs), values_all, precision=HIGH).reshape(2 * TOK_DEV, inner)
    mixed = low_back(low(mixed))
    branch = low_back(jnp.dot(mixed, w_out_attn, precision=HIGH))
    return x_group + branch

def expert_apply(expert_in):
    rows, win_one, wout_one = expert_in
    pre_act = low_back(jnp.dot(rows, win_one, precision=HIGH))
    activated = low(jax.nn.gelu(pre_act))
    return low_back(low(jnp.dot(activated, wout_one, precision=HIGH)))

def reference(block_entry_rows, cotangent, gain_one, w_qkv, w_out_attn, rel_bias, gain_two, router, w_in, w_out, routes, slot_order, cont_ids):
    halves = 2 * N_DP
    slot_id, kept, source, filled = jax.vmap(slot_table)(routes.reshape(halves, TOK_DEV, 2), slot_order)
    base = jnp.arange(halves, dtype=jnp.int32)
    slot_global = (slot_id + base[:, None] * (EXPERTS * CAP)).reshape(TOKENS, 2)
    kept_rows = kept.reshape(TOKENS, 2).astype(jnp.float32)
    source_global = (source + base[:, None] * (2 * TOK_DEV)).reshape(-1)
    filled_rows = filled.reshape(-1).astype(jnp.float32)

    def forward(x_in, gain_a, wqkv_in, wout_attn_in, bias_in, gain_b, router_in, win_in, wout_in):

        def run_group(group_in):
            return attend_group(group_in, gain_a, wqkv_in, wout_attn_in, bias_in)
        groups = x_in.reshape(N_DP, 2 * TOK_DEV, MODEL_WIDTH)
        hidden_activation = lax.map(jax.checkpoint(run_group), (groups, cont_ids)).reshape(TOKENS, MODEL_WIDTH)
        normed = low(rms_norm(hidden_activation, gain_b))
        logits = low_back(jnp.dot(normed, router_in, precision=HIGH))
        chosen = jnp.take_along_axis(logits, routes, axis=1)
        gates = jax.nn.softmax(chosen, axis=1)
        sent = low_back(normed[source_global // 2] * filled_rows[:, None])
        by_expert = sent.reshape(halves, EXPERTS, CAP, MODEL_WIDTH).transpose(1, 0, 2, 3).reshape(EXPERTS, halves * CAP, MODEL_WIDTH)
        returned = lax.map(jax.checkpoint(expert_apply), (by_expert, win_in, wout_in))
        returned = returned.reshape(EXPERTS, halves, CAP, MODEL_WIDTH).transpose(1, 0, 2, 3).reshape(halves * EXPERTS * CAP, MODEL_WIDTH)
        picked = returned[slot_global] * kept_rows[..., None]
        return hidden_activation + lax.optimization_barrier(jnp.sum(gates[..., None] * picked, axis=1))
    floats = (block_entry_rows.astype(jnp.float32), gain_one, w_qkv.astype(jnp.float32), w_out_attn.astype(jnp.float32), rel_bias, gain_two, router.astype(jnp.float32), w_in.astype(jnp.float32), w_out.astype(jnp.float32))
    output, pullback = jax.vjp(forward, *floats)
    grads = pullback(cotangent.astype(jnp.float32))
    return (output, grads[0], grads[2], grads[3], grads[4], grads[1], grads[5], grads[6], grads[7], grads[8])
```

```python
import jax
import jax.numpy as jnp
from jax import lax
from jax.experimental import pallas as pl
from jax.experimental.pallas import tpu as pltpu
from jax.sharding import PartitionSpec as P

MODEL_WIDTH = 768
HEAD = 64
NB = 32
BUCKET = 32


EPS = 1e-06
NEG = -1e30


def from_behind(x, axis, by):
    count = lax.axis_size(axis)
    pairs = [(i, i + by) for i in range(count) if 0 <= i + by < count]
    return lax.ppermute(x, axis, pairs)


def feature_gather(values):
    return lax.all_gather(values, "mx", axis=1, tiled=True)


def feature_sum(values):
    return lax.psum_scatter(
        values.astype(jnp.bfloat16), "mx", scatter_dimension=1, tiled=True
    ).astype(jnp.float32)


def row_dot_total(values):
    return lax.psum(values, "mx")


def expert_swap(values):
    return lax.all_to_all(values, "dp", split_axis=0, concat_axis=0, tiled=True)


def slot_table(route_rows, order, experts, cap_rows):
    flat = route_rows.reshape(-1)
    ranked = flat[order]
    one_hot = (ranked[:, None] == jnp.arange(experts, dtype=jnp.int32)[None, :]).astype(jnp.int32)
    before = jnp.cumsum(one_hot, axis=0) - one_hot
    rank_sorted = jnp.sum(before * one_hot, axis=1)
    ranking = jnp.zeros_like(flat).at[order].set(rank_sorted)
    kept = ranking < cap_rows
    slot_id = flat * cap_rows + jnp.minimum(ranking, cap_rows - 1)
    target = jnp.where(kept, slot_id, experts * cap_rows)
    source = (
        jnp.zeros((experts * cap_rows,), jnp.int32)
        .at[target]
        .set(jnp.arange(flat.shape[0], dtype=jnp.int32), mode="drop")
    )
    filled = jnp.zeros((experts * cap_rows,), jnp.int32).at[target].set(1, mode="drop")
    return (slot_id, kept, source, filled)


SPAN = 256
WIDE = pltpu.CompilerParams(vmem_limit_bytes=50 * 1024 * 1024)


def iota(shape, dim):
    return lax.broadcasted_iota(jnp.int32, shape, dim)


def dot(a, b, dims=((1,), (0,))):
    return lax.dot_general(a, b, (dims, ((), ())), preferred_element_type=jnp.float32)


NT = ((1,), (1,))
TN = ((0,), (0,))


def fill_bias(near_ref, far_ref, table_ref):
    low = (iota((BUCKET, SPAN), 1) & (BUCKET - 1)) >= iota((BUCKET, SPAN), 0)
    for c in range(table_ref.shape[0] // BUCKET):
        table_ref[c * BUCKET : (c + 1) * BUCKET, :] = jnp.where(
            low, near_ref[0, c : c + 1, :], far_ref[0, c : c + 1, :]
        )


def split_bias(table_ref, count):
    table = table_ref[:count, :]
    high = table.astype(jnp.bfloat16)
    return high, (table - high.astype(jnp.float32)).astype(jnp.bfloat16)


def attend_kernel(
    cont_ref, q_ref, k_ref, v_ref, kp_ref, vp_ref, first_ref, near_ref, far_ref,
    o_ref, log_ref, table, key_own, key_prev, val_own, val_prev,
):
    count = q_ref.shape[1]
    cont = cont_ref[0] == 1
    fill_bias(near_ref, far_ref, table)
    key_own[...] = k_ref[...].T
    ones = jnp.ones((16, count), jnp.bfloat16)
    val_own[:HEAD, :] = v_ref[...]
    val_own[HEAD:, :] = ones

    def finish(o, top, cols):
        total = o[HEAD : HEAD + 1, :]
        o_ref[:, cols] = (o[:HEAD, :] / total).astype(jnp.bfloat16)
        log_ref[0, :, cols] = top + jnp.log(total)

    @pl.when(jnp.logical_not(cont))
    def _():
        for b in range(count // SPAN):
            cols = slice(b * SPAN, (b + 1) * SPAN)
            keys = (b + 1) * SPAN
            q = q_ref[:, cols] * jnp.bfloat16(HEAD**-0.5)
            s = dot(key_own[:keys, :], q) + table[count - b * SPAN : count + SPAN, :]
            s = jnp.where(iota((keys, SPAN), 0) <= iota((keys, SPAN), 1) + b * SPAN, s, NEG)
            top = jnp.max(s, axis=0, keepdims=True)
            p = jnp.exp(s - top).astype(jnp.bfloat16)
            finish(dot(val_own[:, :keys], p), top, cols)

    @pl.when(cont)
    def _():
        high, rest = split_bias(table, count)
        key_prev[:, :SPAN] = high
        key_prev[:, SPAN : 2 * SPAN] = rest
        key_prev[:, 2 * SPAN :] = kp_ref[...].T
        val_prev[:HEAD, :] = vp_ref[...]
        val_prev[HEAD:, :] = ones
        for b in range(count // SPAN):
            cols = slice(b * SPAN, (b + 1) * SPAN)
            start = max(b - 1, 0) * SPAN
            rows = slice(start, (b + 1) * SPAN)
            keys = (b + 1) * SPAN - start
            q = q_ref[:, cols] * jnp.bfloat16(HEAD**-0.5)
            first = first_ref[:, cols]
            place = iota((1, SPAN), 1) + b * SPAN
            hot = (iota((SPAN, SPAN), 0) == place - first).astype(jnp.bfloat16)
            s1 = dot(key_prev[...], jnp.concatenate([hot, hot, q], axis=0))
            s2 = dot(key_own[rows, :], q) + table[count + start - b * SPAN : count + SPAN, :]
            at = iota((keys, SPAN), 0) + start
            s2 = jnp.where((at <= place) & (at >= first), s2, NEG)
            top = jnp.maximum(
                jnp.max(s1, axis=0, keepdims=True), jnp.max(s2, axis=0, keepdims=True)
            )
            p1 = jnp.exp(s1 - top).astype(jnp.bfloat16)
            p2 = jnp.exp(s2 - top).astype(jnp.bfloat16)
            finish(dot(val_prev[...], p1) + dot(val_own[:, rows], p2), top, cols)


def attend(cont, proj, prev, first, near, far):
    heads, count = proj.shape[0] // (3 * HEAD), proj.shape[1]
    part = lambda k: pl.BlockSpec((HEAD, count), lambda h: (h + k * heads, 0))
    table = pl.BlockSpec((1,) + near.shape[1:], lambda h: (h, 0, 0))
    return pl.pallas_call(
        attend_kernel,
        grid=(heads,),
        in_specs=[
            pl.BlockSpec(memory_space=pltpu.SMEM),
            part(0), part(1), part(2), part(0), part(1),
            pl.BlockSpec((1, count), lambda h: (0, 0)),
            table, table,
        ],
        out_specs=[part(0), pl.BlockSpec((1, 1, count), lambda h: (h, 0, 0))],
        out_shape=[
            jax.ShapeDtypeStruct((heads * HEAD, count), jnp.bfloat16),
            jax.ShapeDtypeStruct((heads, 1, count), jnp.float32),
        ],
        scratch_shapes=[
            pltpu.VMEM((2 * count, SPAN), jnp.float32),
            pltpu.VMEM((count, HEAD), jnp.bfloat16),
            pltpu.VMEM((count, HEAD + 2 * SPAN), jnp.bfloat16),
            pltpu.VMEM((HEAD + 16, count), jnp.bfloat16),
            pltpu.VMEM((HEAD + 16, count), jnp.bfloat16),
        ],
        compiler_params=WIDE,
        name="attend",
    )(cont, proj, proj, proj, prev, prev, first, near, far)


def attend_back_kernel(
    cont_ref, q_ref, k_ref, v_ref, kp_ref, vp_ref, first_ref, near_ref, far_ref, o_ref, log_ref, do_ref,
    dq_ref, dk_ref, dv_ref, dkp_ref, dvp_ref, sum_near_ref, sum_far_ref,
    table, key_own, key_prev, val_own, val_prev, q_cat, q_nat, do_nat, hot_nat, dtable, dq, dk, dv,
):
    count = q_ref.shape[1]
    blocks = count // SPAN
    cont = cont_ref[0] == 1
    fill_bias(near_ref, far_ref, table)
    key_own[...] = k_ref[...].T
    val_own[...] = v_ref[...].T
    q = q_ref[...] * jnp.bfloat16(HEAD**-0.5)
    q_cat[2 * SPAN :, :] = q
    q_nat[...] = q.T
    do_nat[...] = do_ref[...].T
    dtable[...] = jnp.zeros_like(dtable)
    dq[...] = jnp.zeros_like(dq)
    dk[...] = jnp.zeros_like(dk)
    dv[...] = jnp.zeros_like(dv)
    delta = jnp.sum(
        do_ref[...].astype(jnp.float32) * o_ref[...].astype(jnp.float32), axis=0, keepdims=True
    )

    def tile(kb, qb):
        rows = slice(kb * SPAN, (kb + 1) * SPAN)
        cols = slice(qb * SPAN, (qb + 1) * SPAN)
        where = slice(count + (kb - qb) * SPAN, count + (kb - qb + 1) * SPAN)
        s = dot(key_own[rows, :], q_cat[2 * SPAN :, cols]) + table[where, :]
        at = iota((SPAN, SPAN), 0) + kb * SPAN
        live = (at <= iota((SPAN, SPAN), 1) + qb * SPAN) & (at >= first_ref[:, cols])
        p = jnp.exp(jnp.where(live, s, NEG) - log_ref[0, :, cols])
        dp = dot(val_own[rows, :], do_ref[:, cols])
        ds = p * (dp - delta[:, cols])
        dtable[where, :] += ds
        ds = ds.astype(jnp.bfloat16)
        dk[rows, :] += dot(ds, q_nat[cols, :])
        dv[rows, :] += dot(p.astype(jnp.bfloat16), do_nat[cols, :])
        dq[:, cols] += dot(k_ref[:, rows], ds)

    for kb in range(blocks):
        for qb in range(kb, min(kb + 2, blocks)):
            tile(kb, qb)

    @pl.when(jnp.logical_not(cont))
    def _():
        for kb in range(blocks):
            for qb in range(kb + 2, blocks):
                tile(kb, qb)

    @pl.when(cont)
    def _():
        high, rest = split_bias(table, count)
        key_prev[:, :SPAN] = high
        key_prev[:, SPAN : 2 * SPAN] = rest
        key_prev[:, 2 * SPAN :] = kp_ref[...].T
        val_prev[...] = vp_ref[...].T
        hot = (iota((SPAN, count), 0) == iota((1, count), 1) - first_ref[...]).astype(jnp.bfloat16)
        q_cat[:SPAN, :] = hot
        q_cat[SPAN : 2 * SPAN, :] = hot
        hot_nat[...] = hot.T

        for kb in range(blocks):
            rows = slice(kb * SPAN, (kb + 1) * SPAN)
            s = dot(key_prev[rows, :], q_cat[...])
            p = jnp.exp(s - log_ref[0])
            dp = dot(val_prev[rows, :], do_ref[...])
            ds = (p * (dp - delta)).astype(jnp.bfloat16)
            dkp_ref[:, rows] = dot(ds, q_nat[...]).astype(jnp.bfloat16).T
            dvp_ref[:, rows] = dot(p.astype(jnp.bfloat16), do_nat[...]).astype(jnp.bfloat16).T
            dtable[rows, :] += dot(ds, hot_nat[...])
            dq[...] += dot(kp_ref[:, rows], ds)

    dq_ref[...] = (dq[...] * HEAD**-0.5).astype(jnp.bfloat16)
    dk_ref[...] = dk[...].astype(jnp.bfloat16).T
    dv_ref[...] = dv[...].astype(jnp.bfloat16).T
    low = (iota((BUCKET, SPAN), 1) & (BUCKET - 1)) >= iota((BUCKET, SPAN), 0)
    for c in range(2 * count // BUCKET):
        part = dtable[c * BUCKET : (c + 1) * BUCKET, :]
        near = jnp.sum(jnp.where(low, part, 0.0), axis=0, keepdims=True)
        sum_near_ref[0, c : c + 1, :] = near
        sum_far_ref[0, c : c + 1, :] = jnp.sum(part, axis=0, keepdims=True) - near


def attend_back(cont, proj, prev, first, near, far, o, log, do):
    heads, count = proj.shape[0] // (3 * HEAD), proj.shape[1]
    part = lambda k: pl.BlockSpec((HEAD, count), lambda h: (h + k * heads, 0))
    table = pl.BlockSpec((1,) + near.shape[1:], lambda h: (h, 0, 0))
    grad = jax.ShapeDtypeStruct((heads * HEAD, count), jnp.bfloat16)
    sums = jax.ShapeDtypeStruct(near.shape, jnp.float32)
    return pl.pallas_call(
        attend_back_kernel,
        grid=(heads,),
        in_specs=[
            pl.BlockSpec(memory_space=pltpu.SMEM),
            part(0), part(1), part(2), part(0), part(1),
            pl.BlockSpec((1, count), lambda h: (0, 0)),
            table, table, part(0),
            pl.BlockSpec((1, 1, count), lambda h: (h, 0, 0)),
            part(0),
        ],
        out_specs=[part(0)] * 5 + [table] * 2,
        out_shape=[grad] * 5 + [sums] * 2,
        scratch_shapes=[
            pltpu.VMEM((2 * count, SPAN), jnp.float32),
            pltpu.VMEM((count, HEAD), jnp.bfloat16),
            pltpu.VMEM((count, HEAD + 2 * SPAN), jnp.bfloat16),
            pltpu.VMEM((count, HEAD), jnp.bfloat16),
            pltpu.VMEM((count, HEAD), jnp.bfloat16),
            pltpu.VMEM((HEAD + 2 * SPAN, count), jnp.bfloat16),
            pltpu.VMEM((count, HEAD), jnp.bfloat16),
            pltpu.VMEM((count, HEAD), jnp.bfloat16),
            pltpu.VMEM((count, SPAN), jnp.bfloat16),
            pltpu.VMEM((2 * count, SPAN), jnp.float32),
            pltpu.VMEM((HEAD, count), jnp.float32),
            pltpu.VMEM((count, HEAD), jnp.float32),
            pltpu.VMEM((count, HEAD), jnp.float32),
        ],
        compiler_params=WIDE,
        name="attend_back",
    )(cont, proj, proj, proj, prev, prev, first, near, far, o, log, do)


def bias_levels(bias, count):
    rows, lanes = 2 * count // BUCKET, SPAN // BUCKET
    step = jnp.arange(lanes)[None, :] - jnp.arange(rows)[:, None] + rows // 2
    names = jnp.arange(NB)
    near_hot = (jnp.clip(step, 0, NB - 1)[..., None] == names).astype(jnp.float32)
    far_hot = (jnp.clip(step - 1, 0, NB - 1)[..., None] == names).astype(jnp.float32)
    return near_hot, far_hot


def bias_tables(bias, count):
    out = []
    for hot in bias_levels(bias, count):
        level = jnp.sum(hot[None] * bias[:, None, None, :], axis=-1)
        out.append(jnp.repeat(level, BUCKET, axis=2))
    return out


def bias_totals(sum_near, sum_far, count):
    total = 0.0
    for hot, sums in zip(bias_levels(None, count), (sum_near, sum_far)):
        level = jnp.sum(sums.reshape(sums.shape[0], sums.shape[1], -1, BUCKET), axis=-1)
        total = total + jnp.sum(level[..., None] * hot[None], axis=(1, 2))
    return total


def root_mean_square_pullback(normalized_gradient, local_gain, unit_scaled_input, inverse_norm):
    unit_scaled_gradient = normalized_gradient * local_gain
    norm_gain_gradient = jnp.sum(normalized_gradient * unit_scaled_input, axis=0)
    normalized_dot_product = (
        row_dot_total(jnp.sum(unit_scaled_gradient * unit_scaled_input, axis=1, keepdims=True))
        / MODEL_WIDTH
    )
    return (
        inverse_norm * (unit_scaled_gradient - unit_scaled_input * normalized_dot_product),
        norm_gain_gradient,
    )


def body(
    block_entry_rows,
    cotangent,
    gain_one,
    w_qkv,
    w_out_attn,
    rel_bias,
    gain_two,
    router,
    w_in,
    w_out,
    routes,
    slot_order,
    cont_ids,
):
    tok_len = block_entry_rows.shape[0]
    feat_local = block_entry_rows.shape[1]
    feat_index = lax.axis_index("mx")
    feat_start = feat_index * feat_local
    is_cont = lax.axis_index("my") == 1
    experts = router.shape[1]
    per_dev = w_in.shape[0]
    owners = experts // per_dev
    cap_rows = 2 * tok_len // experts
    inner_local = w_qkv.shape[2]
    heads_local = inner_local // HEAD
    qkv_full, proj_full, win_full, wout_full = (
        lax.all_gather(w_qkv, "my", axis=0, tiled=True),
        lax.all_gather(w_out_attn, "my", axis=1, tiled=True),
        lax.all_gather(w_in, "my", axis=1, tiled=True),
        lax.all_gather(w_out, "my", axis=2, tiled=True),
    )
    qkv_flat = qkv_full.reshape(qkv_full.shape[0], 3 * inner_local)
    x_full = feature_gather(block_entry_rows).astype(jnp.float32)
    first_inverse_norm = lax.rsqrt(jnp.mean(x_full * x_full, axis=1, keepdims=True) + EPS)
    normed_one = (x_full * first_inverse_norm * gain_one).astype(jnp.bfloat16)
    projected = lax.dot_general(
        qkv_flat, normed_one, (((0,), (1,)), ((), ())), preferred_element_type=jnp.float32
    ).astype(jnp.bfloat16)
    earlier = from_behind(projected[inner_local:], "my", 1)
    index = jnp.arange(tok_len, dtype=jnp.int32)
    same_seg = cont_ids[0][:, None] == cont_ids[0][None, :]
    first_pos = jnp.min(jnp.where(same_seg, index[:, None], tok_len), axis=0, keepdims=True)
    first_pos = jnp.where(is_cont, first_pos, 0)
    bias_local = lax.dynamic_slice_in_dim(rel_bias, feat_index * heads_local, heads_local, 0)
    near, far = bias_tables(bias_local, tok_len)
    cont_flag = is_cont.astype(jnp.int32).reshape(1)
    geometry = (cont_flag, projected, earlier, first_pos, near, far)
    mixed_rows, log_sums = attend(*geometry)
    mixed = mixed_rows.T
    branch = feature_sum(jnp.dot(mixed, proj_full, preferred_element_type=jnp.float32))
    hidden_activation = block_entry_rows.astype(jnp.float32) + branch
    second_inverse_norm = lax.rsqrt(
        row_dot_total(jnp.sum(hidden_activation * hidden_activation, axis=1, keepdims=True))
        / MODEL_WIDTH
        + EPS
    )
    local_gain_second = lax.dynamic_slice_in_dim(gain_two, feat_start, feat_local, 0)
    second_unit_scaled = hidden_activation * second_inverse_norm
    second_normalized = (second_unit_scaled * local_gain_second).astype(jnp.bfloat16)
    normed_full = feature_gather(second_normalized)
    logits = jnp.dot(normed_full, router, preferred_element_type=jnp.float32)
    route_hot = routes[:, :, None] == jnp.arange(experts, dtype=jnp.int32)[None, None, :]
    chosen = jnp.sum(jnp.where(route_hot, logits[:, None, :], 0.0), axis=2)
    gates = jax.nn.softmax(chosen, axis=1)
    slot_id, kept, source, filled = slot_table(routes, slot_order[0], experts, cap_rows)
    kept_rows = kept.reshape(tok_len, 2).astype(jnp.float32)
    slot_rows = slot_id.reshape(tok_len, 2)
    fill_mask = filled[:, None].astype(jnp.bfloat16)
    outgoing = jnp.take(second_normalized, source // 2, axis=0) * fill_mask
    arrived = expert_swap(outgoing.reshape(owners, per_dev * cap_rows, feat_local))
    rows_full = feature_gather(arrived.reshape(-1, feat_local)).reshape(
        owners, per_dev, cap_rows, -1
    )
    pre_act = jnp.einsum("sjcd,jdf->sjcf", rows_full, win_full, preferred_element_type=jnp.float32)
    activated = jax.nn.gelu(pre_act).astype(jnp.bfloat16)
    partial_out = jnp.einsum(
        "sjcf,jfd->sjcd", activated, wout_full, preferred_element_type=jnp.float32
    )
    expert_out = feature_sum(partial_out.reshape(owners * per_dev * cap_rows, -1)).astype(
        jnp.bfloat16
    )
    returned = expert_swap(expert_out.reshape(owners, per_dev * cap_rows, feat_local)).reshape(
        experts * cap_rows, feat_local
    )
    picked = jnp.take(returned, slot_rows, axis=0).astype(jnp.float32) * kept_rows[..., None]
    out_rows = hidden_activation + jnp.sum(gates[..., None] * picked, axis=1)
    grad_out = cotangent.astype(jnp.float32)
    gate_grad = row_dot_total(jnp.sum(grad_out[:, None, :] * picked, axis=2))
    back_rows = (
        (gates[..., None] * grad_out[:, None, :] * kept_rows[..., None])
        .astype(jnp.bfloat16)
        .reshape(2 * tok_len, feat_local)
    )
    back_sent = jnp.take(back_rows, source, axis=0) * fill_mask
    back_arrived = expert_swap(back_sent.reshape(owners, per_dev * cap_rows, feat_local))
    back_full = feature_gather(back_arrived.reshape(-1, feat_local)).reshape(
        owners, per_dev, cap_rows, -1
    )
    act_grad = jnp.einsum(
        "sjcd,jfd->sjcf", back_full, wout_full, preferred_element_type=jnp.float32
    )
    grad_wout = jnp.einsum(
        "sjcf,sjcd->jfd", activated, back_full, preferred_element_type=jnp.float32
    )
    gelu_value, gelu_pull = jax.vjp(jax.nn.gelu, pre_act)
    pre_grad = gelu_pull(act_grad)[0].astype(jnp.bfloat16)
    rows_part = jnp.einsum("sjcf,jdf->sjcd", pre_grad, win_full, preferred_element_type=jnp.float32)
    rows_grad = feature_sum(rows_part.reshape(owners * per_dev * cap_rows, -1)).astype(jnp.bfloat16)
    grad_win = jnp.einsum("sjcd,sjcf->jdf", rows_full, pre_grad, preferred_element_type=jnp.float32)
    rows_back = expert_swap(rows_grad.reshape(owners, per_dev * cap_rows, feat_local)).reshape(
        experts * cap_rows, feat_local
    )
    normalized_gradient = jnp.sum(
        jnp.take(rows_back, slot_rows, axis=0).astype(jnp.float32) * kept_rows[..., None], axis=1
    )
    gate_dot = jnp.sum(gates * gate_grad, axis=1, keepdims=True)
    chosen_grad = gates * (gate_grad - gate_dot)
    logit_grad = jnp.sum(jnp.where(route_hot, chosen_grad[:, :, None], 0.0), axis=1).astype(
        jnp.bfloat16
    )
    router_rows = lax.dynamic_slice_in_dim(router, feat_start, feat_local, 0)
    normalized_gradient = normalized_gradient + lax.dot_general(
        logit_grad, router_rows, (((1,), (1,)), ((), ())), preferred_element_type=jnp.float32
    )
    grad_router_rows = lax.dot_general(
        second_normalized, logit_grad, (((0,), (0,)), ((), ())), preferred_element_type=jnp.float32
    )
    second_norm_pullback, second_gain_gradient = root_mean_square_pullback(
        normalized_gradient, local_gain_second, second_unit_scaled, second_inverse_norm
    )
    hidden_grad = grad_out + second_norm_pullback
    hidden_full = feature_gather(hidden_grad.astype(jnp.bfloat16))
    mixed_grad = lax.dot_general(
        hidden_full, proj_full, (((1,), (1,)), ((), ())), preferred_element_type=jnp.float32
    ).astype(jnp.bfloat16)
    grad_proj = lax.dot_general(
        mixed, hidden_full, (((0,), (0,)), ((), ())), preferred_element_type=jnp.float32
    )
    (
        query_grad, keys_grad, vals_grad, keys_back, vals_back, near_sums, far_sums
    ) = attend_back(*geometry, mixed_rows, log_sums, mixed_grad.T)
    bias_grad = bias_totals(near_sums, far_sums, tok_len)
    returned_grad = from_behind(jnp.concatenate([keys_back, vals_back], axis=0), "my", -1)
    own_grad = (
        jnp.concatenate([keys_grad, vals_grad], axis=0).astype(jnp.float32)
        + returned_grad.astype(jnp.float32)
    ).astype(jnp.bfloat16)
    proj_grad = jnp.concatenate([query_grad, own_grad], axis=0).T
    grad_qkv = lax.dot_general(
        normed_one, proj_grad, (((0,), (0,)), ((), ())), preferred_element_type=jnp.float32
    ).reshape(qkv_full.shape[0], 3, inner_local)
    first_normalized_gradient = feature_sum(
        lax.dot_general(
            proj_grad, qkv_flat, (((1,), (1,)), ((), ())), preferred_element_type=jnp.float32
        )
    )
    local_gain_first = lax.dynamic_slice_in_dim(gain_one, feat_start, feat_local, 0)
    first_unit_scaled = block_entry_rows.astype(jnp.float32) * first_inverse_norm
    first_norm_pullback, first_gain_gradient = root_mean_square_pullback(
        first_normalized_gradient, local_gain_first, first_unit_scaled, first_inverse_norm
    )
    input_grad = hidden_grad + first_norm_pullback
    grad_qkv, grad_proj, grad_win, grad_wout = (
        lax.psum_scatter(
            grad_qkv.astype(jnp.bfloat16), "my", scatter_dimension=0, tiled=True
        ).astype(jnp.float32),
        lax.psum_scatter(
            grad_proj.astype(jnp.bfloat16), "my", scatter_dimension=1, tiled=True
        ).astype(jnp.float32),
        lax.psum_scatter(
            grad_win.astype(jnp.bfloat16), "my", scatter_dimension=1, tiled=True
        ).astype(jnp.float32),
        lax.psum_scatter(
            grad_wout.astype(jnp.bfloat16), "my", scatter_dimension=2, tiled=True
        ).astype(jnp.float32),
    )
    grad_qkv, grad_proj = (
        lax.psum(grad_qkv.astype(jnp.bfloat16), "dp").astype(jnp.float32),
        lax.psum(grad_proj.astype(jnp.bfloat16), "dp").astype(jnp.float32),
    )
    full_bias = lax.dynamic_update_slice_in_dim(
        jnp.zeros(rel_bias.shape, jnp.float32), bias_grad, feat_index * heads_local, 0
    )
    full_gain_one = lax.dynamic_update_slice_in_dim(
        jnp.zeros(gain_one.shape, jnp.float32), first_gain_gradient, feat_start, 0
    )
    full_gain_two = lax.dynamic_update_slice_in_dim(
        jnp.zeros(gain_two.shape, jnp.float32), second_gain_gradient, feat_start, 0
    )
    full_router = lax.dynamic_update_slice_in_dim(
        jnp.zeros(router.shape, jnp.float32), grad_router_rows, feat_start, 0
    )
    full_bias, full_gain_one, full_gain_two, full_router = lax.psum(
        (full_bias, full_gain_one, full_gain_two, full_router), ("dp", "mx", "my")
    )
    return (
        out_rows,
        input_grad,
        grad_qkv,
        grad_proj,
        full_bias,
        full_gain_one,
        full_gain_two,
        full_router,
        grad_win,
        grad_wout,
    )


def solution(mesh):
    return jax.shard_map(
        body,
        mesh=mesh,
        in_specs=(
            P(("dp", "my"), "mx"),
            P(("dp", "my"), "mx"),
            P(),
            P("my", None, "mx"),
            P("mx", "my"),
            P(),
            P(),
            P(),
            P("dp", "my", "mx"),
            P("dp", "mx", "my"),
            P(("dp", "my"), None),
            P(("dp", "my"), None),
            P("dp", None),
        ),
        out_specs=(
            P(("dp", "my"), "mx"),
            P(("dp", "my"), "mx"),
            P("my", None, "mx"),
            P("mx", "my"),
            P(),
            P(),
            P(),
            P(),
            P("dp", "my", "mx"),
            P("dp", "mx", "my"),
        ),
        check_vma=False,
    )
```

```python
import jax
import jax.numpy as jnp
from jax import lax
from jax.experimental import pallas as pl
from jax.experimental.pallas import tpu as pltpu
from jax.sharding import PartitionSpec as P

HEAD = 64
NB = 32
BUCKET = 32
SPAN = 256
TAIL = 16

EPS = 1e-06
NEG = -1e30

BF = jnp.bfloat16
F32 = jnp.float32
NN = ((1,), (0,))
NT = ((1,), (1,))
TN = ((0,), (0,))
WIDE = pltpu.CompilerParams(vmem_limit_bytes=50 * 1024 * 1024)
VMEM = pl.BlockSpec(memory_space=pltpu.VMEM)
SMEM = pl.BlockSpec(memory_space=pltpu.SMEM)


def swap(values, axis, step):
    return lax.ppermute(values, axis, [(i, i ^ step) for i in range(lax.axis_size(axis))])


def spread(values, axis):
    return [values] + [swap(values, axis, s) for s in range(1, lax.axis_size(axis))]


def exchange(blocks, axis):
    return [blocks[0]] + [swap(blocks[s], axis, s) for s in range(1, len(blocks))]


def cube_sum(values, axis, dtype):
    for bit in range((lax.axis_size(axis) - 1).bit_length()):
        sent = values.astype(dtype)
        values = sent.astype(F32) + swap(sent, axis, 1 << bit).astype(F32)
    return values


def iota(shape, dim):
    return lax.broadcasted_iota(jnp.int32, shape, dim)


def dot(a, b, dims=NN):
    return lax.dot_general(a, b, (dims, ((), ())), preferred_element_type=F32)


def shape_of(dims, dtype):
    return jax.ShapeDtypeStruct(dims, dtype)


def chunked(rows):
    return pl.BlockSpec((rows, SPAN), lambda c: (0, c))


def whole(*dims):
    return pl.BlockSpec(dims, lambda c: (0,) * len(dims))


def column_sum(values):
    return jnp.sum(values, axis=0, keepdims=True)


def token_sums(values):
    return dot(jnp.ones((8, values.shape[1]), BF), values.astype(BF), NT)


def part_rows(index, size):
    return pl.ds(pl.multiple_of(index * size, 64), size)


def slots_kernel(cap, base_ref, routes_ref, order_ref, slots_ref, hot):
    tokens, pairs = hot.shape
    experts = base_ref.shape[0]
    token = lax.shift_right_logical(order_ref[...], 1)
    second = (order_ref[...] & 1) == 1
    hot[...] = (iota((tokens, pairs), 0) == token).astype(BF)
    named = iota((experts, tokens), 0)
    chosen = jnp.where(
        second,
        dot((named == routes_ref[1:2, :]).astype(BF), hot[...]),
        dot((named == routes_ref[0:1, :]).astype(BF), hot[...]),
    )
    place = iota(chosen.shape, 1)
    upto, step = chosen, 1
    while step < pairs:
        upto = upto + jnp.where(place >= step, pltpu.roll(upto, step, 1), 0.0)
        step *= 2
    rank = column_sum((upto - chosen) * chosen)
    slot = column_sum(chosen * base_ref[...]) + rank
    kept = (rank < cap).astype(F32)
    high = jnp.floor(slot * (1 / 64))
    low = slot - 64 * high
    own = kept * second.astype(F32)
    rows = [value * side for side in (kept - own, own) for value in (high, low, 1.0)]
    rows = jnp.concatenate(rows + [rows[0] * 0.0] * 10, axis=0).astype(BF)
    found = dot(rows, hot[...], NT)
    for k in range(2):
        at = found[3 * k : 3 * k + 1, :] * 64 + found[3 * k + 1 : 3 * k + 2, :]
        at = jnp.where(found[3 * k + 2 : 3 * k + 3, :] > 0.5, at, -1.0)
        slots_ref[k : k + 1, :] = at.astype(jnp.int32)


def slot_rows(base, routes, order, cap):
    tokens = routes.shape[1]
    return pl.pallas_call(
        lambda *refs: slots_kernel(cap, *refs),
        in_specs=[VMEM] * 3,
        out_specs=VMEM,
        out_shape=shape_of((2, tokens), jnp.int32),
        scratch_shapes=[pltpu.VMEM((tokens, 2 * tokens), BF)],
        compiler_params=WIDE,
        name="slots",
    )(base, routes, order)


def project_kernel(me_ref, *refs):
    pieces = refs[:-6]
    w_ref, gain_ref, full_ref, normed_ref, proj_ref, inverse_ref = refs[-6:]
    size = pieces[0].shape[0]
    for s, piece in enumerate(pieces):
        full_ref[part_rows(me_ref[0] ^ s, size), :] = piece[...]
    x = full_ref[...].astype(F32)
    inverse = lax.rsqrt(jnp.mean(x * x, axis=0, keepdims=True) + EPS)
    normed = (x * inverse * gain_ref[...]).astype(BF)
    normed_ref[...] = normed
    inverse_ref[...] = inverse
    proj_ref[...] = dot(w_ref[...], normed, TN).astype(BF)


def project(me, pieces, w, gain):
    size, tokens = pieces[0].shape
    width, inner = w.shape
    return pl.pallas_call(
        project_kernel,
        grid=(tokens // SPAN,),
        in_specs=[SMEM] + [chunked(size)] * len(pieces) + [whole(width, inner), whole(width, 1)],
        out_specs=[chunked(width), chunked(width), chunked(inner), chunked(1)],
        out_shape=[
            shape_of((width, tokens), BF),
            shape_of((width, tokens), BF),
            shape_of((inner, tokens), BF),
            shape_of((1, tokens), F32),
        ],
        compiler_params=WIDE,
        name="project",
    )(me, *pieces, w, gain)


def hot_slots(slots_ref, k, block, size, cols=slice(None)):
    at = slots_ref[k : k + 1, cols]
    return (iota((size, at.shape[1]), 0) + block * size == at).astype(BF)


def enter_kernel(parts, me_ref, *refs):
    o_refs, w_refs, refs = refs[:parts], refs[parts : 2 * parts], refs[2 * parts :]
    (x_ref, gain_ref, router_ref, routes_ref, slots_ref) = refs[:5]
    (own_ref, inverse_ref, normed_ref, gates_ref) = refs[5:9]
    row_refs, h_all = refs[9:-1], refs[-1]
    size = own_ref.shape[0]
    tokens = x_ref.shape[1]
    width = x_ref.shape[0]
    experts = router_ref.shape[1]
    w = jnp.concatenate([ref[...] for ref in w_refs], axis=0)
    for c in range(tokens // SPAN):
        cols = slice(c * SPAN, (c + 1) * SPAN)
        o = jnp.concatenate([ref[:, cols] for ref in o_refs], axis=0)
        h = x_ref[:, cols].astype(F32) + dot(w, o, TN)
        h_all[:, cols] = h
        inverse = lax.rsqrt(jnp.mean(h * h, axis=0, keepdims=True) + EPS)
        normed = (h * inverse * gain_ref[...]).astype(BF)
        inverse_ref[:, cols] = inverse
        normed_ref[:, cols] = normed
        logits = dot(router_ref[...], normed, TN)
        named = iota((experts, SPAN), 0)
        one, two = [
            column_sum(jnp.where(named == routes_ref[k : k + 1, cols], logits, 0.0)) for k in range(2)
        ]
        top = jnp.maximum(one, two)
        one, two = jnp.exp(one - top), jnp.exp(two - top)
        total = one + two
        gates_ref[0:1, cols] = one / total
        gates_ref[1:2, cols] = two / total
    own_ref[...] = h_all[part_rows(me_ref[0], size), :]
    gate_rows = []
    for k in range(2):
        gate = gates_ref[k : k + 1, :]
        high = gate.astype(BF)
        rest = (gate - high.astype(F32)).astype(BF)
        gate_rows.append(jnp.concatenate([high, rest, jnp.zeros((TAIL - 2, tokens), BF)], axis=0))
    for b, ref in enumerate(row_refs):
        hots = [hot_slots(slots_ref, k, b, ref.shape[1]) for k in range(2)]
        ref[:width, :] = dot(normed_ref[...], hots[0] + hots[1], NT).astype(BF)
        ref[width:, :] = (dot(gate_rows[0], hots[0], NT) + dot(gate_rows[1], hots[1], NT)).astype(BF)


def enter(me, o_pieces, w_pieces, x, gain, router, routes, slots, blocks, block):
    size, tokens = o_pieces[0].shape
    width = x.shape[0]
    parts = len(o_pieces)
    return pl.pallas_call(
        lambda *refs: enter_kernel(parts, *refs),
        in_specs=[SMEM] + [VMEM] * (2 * parts + 5),
        out_specs=[VMEM] * (4 + blocks),
        out_shape=[
            shape_of((width // parts, tokens), F32),
            shape_of((1, tokens), F32),
            shape_of((width, tokens), BF),
            shape_of((2, tokens), F32),
        ]
        + [shape_of((width + TAIL, block), BF)] * blocks,
        scratch_shapes=[pltpu.VMEM((width, tokens), F32)],
        compiler_params=WIDE,
        name="enter",
    )(me, *o_pieces, *w_pieces, x, gain, router, routes, slots)


def send_kernel(parts, me_ref, *refs):
    pieces, slots_ref, full_ref, row_refs = refs[:parts], refs[parts], refs[parts + 1], refs[parts + 2 :]
    size = pieces[0].shape[0]
    for s, piece in enumerate(pieces):
        full_ref[part_rows(me_ref[0] ^ s, size), :] = piece[...]
    for b, ref in enumerate(row_refs):
        hot = hot_slots(slots_ref, 0, b, ref.shape[1]) + hot_slots(slots_ref, 1, b, ref.shape[1])
        ref[...] = dot(full_ref[...], hot, NT).astype(BF)


def send_rows(me, pieces, slots, blocks, block):
    size, tokens = pieces[0].shape
    width = size * len(pieces)
    return pl.pallas_call(
        lambda *refs: send_kernel(len(pieces), *refs),
        in_specs=[SMEM] + [VMEM] * (len(pieces) + 1),
        out_specs=[VMEM] * (1 + blocks),
        out_shape=[shape_of((width, tokens), BF)] + [shape_of((width, block), BF)] * blocks,
        compiler_params=WIDE,
        name="send",
    )(me, *pieces, slots)


def expert_kernel(count, *refs):
    rows, cots = refs[:count], refs[count : 2 * count]
    w_in_ref, w_out_ref = refs[2 * count : 2 * count + 2]
    outs = refs[2 * count + 2 : 3 * count + 2]
    act_ref, pre_ref, sent_ref = refs[3 * count + 2 :]
    width = w_in_ref.shape[0]
    scale = (2 / jnp.pi) ** 0.5
    for b in range(count):
        block = rows[b].shape[1]
        cols = slice(b * block, (b + 1) * block)
        gate = column_sum(rows[b][width : width + 2, :].astype(F32))
        cot = cots[b][...]
        sent_ref[:, cols] = (cot.astype(F32) * gate).astype(BF)
        pre = dot(w_in_ref[...], rows[b][:width, :], TN)
        square = pre * pre
        bend = jnp.tanh(scale * pre * (1 + 0.044715 * square))
        half = 0.5 * (1 + bend)
        act = (pre * half).astype(BF)
        slope = half + 0.5 * pre * (1 - bend * bend) * (scale * (1 + 3 * 0.044715 * square))
        act_ref[:, cols] = act
        back = dot(w_out_ref[...], cot)
        gate_grad = column_sum(act.astype(F32) * back)
        pre_grad = (slope * back * gate).astype(BF)
        pre_ref[:, cols] = pre_grad
        outs[b][:width, :] = dot(w_in_ref[...], pre_grad).astype(BF)
        high = gate_grad.astype(BF)
        rest = (gate_grad - high.astype(F32)).astype(BF)
        outs[b][width:, :] = jnp.concatenate([high, rest, jnp.zeros((TAIL - 2, block), BF)], axis=0)


def expert(rows, cots, w_in, w_out):
    count, block = len(rows), rows[0].shape[1]
    width, hidden = w_in.shape
    return pl.pallas_call(
        lambda *refs: expert_kernel(count, *refs),
        in_specs=[VMEM] * (2 * count + 2),
        out_specs=[VMEM] * (count + 3),
        out_shape=[shape_of((width + TAIL, block), BF)] * count
        + [shape_of((hidden, count * block), BF)] * 2
        + [shape_of((width, count * block), BF)],
        compiler_params=WIDE,
        name="expert",
    )(*rows, *cots, w_in, w_out)


def expert_out_kernel(act_ref, w_out_ref, *outs):
    for b, out in enumerate(outs):
        block = out.shape[1]
        out[...] = dot(w_out_ref[...], act_ref[:, b * block : (b + 1) * block], TN).astype(BF)


def expert_out(act, w_out, count):
    block = act.shape[1] // count
    return pl.pallas_call(
        expert_out_kernel,
        in_specs=[VMEM] * 2,
        out_specs=[VMEM] * count,
        out_shape=[shape_of((w_out.shape[1], block), BF)] * count,
        compiler_params=WIDE,
        name="expert_out",
    )(act, w_out)


def expert_weights_kernel(count, side_ref, *refs):
    rows = refs[:count]
    act_ref, pre_ref, sent_ref, in_keep, in_send, out_keep, out_send = refs[count:]
    half = in_keep.shape[0]
    block = rows[0].shape[1]
    for in_ref, out_ref, side in (
        (in_keep, out_keep, side_ref[0]),
        (in_send, out_send, 1 - side_ref[0]),
    ):
        at = part_rows(side, half)
        total = 0.0
        for b in range(count):
            total = total + dot(rows[b][at, :], pre_ref[:, b * block : (b + 1) * block], NT)
        in_ref[...] = total.astype(in_ref.dtype)
        out_ref[...] = dot(act_ref[...], sent_ref[at, :], NT).astype(out_ref.dtype)


def expert_weights(side, rows, act, pre, sent):
    width, hidden = sent.shape[0], act.shape[0]
    return pl.pallas_call(
        lambda *refs: expert_weights_kernel(len(rows), *refs),
        in_specs=[SMEM] + [VMEM] * (len(rows) + 3),
        out_specs=[VMEM] * 4,
        out_shape=[
            shape_of((width // 2, hidden), F32),
            shape_of((width // 2, hidden), BF),
            shape_of((hidden, width // 2), F32),
            shape_of((hidden, width // 2), BF),
        ],
        compiler_params=WIDE,
        name="expert_weights",
    )(side, *rows, act, pre, sent)


def collect_kernel(blocks, parts, *refs):
    row_refs, w_refs = refs[:blocks], refs[blocks : blocks + parts]
    slots_ref, inverse_ref, gain_ref, normed_ref = refs[blocks + parts : blocks + parts + 4]
    part_ref, small_ref, sums_ref = refs[blocks + parts + 4 : blocks + parts + 7]
    out_refs = refs[blocks + parts + 7 :]
    width = gain_ref.shape[0]
    total = 0.0
    gate_grads = [0.0, 0.0]
    for b, ref in enumerate(row_refs):
        hots = [hot_slots(slots_ref, k, b, ref.shape[1]) for k in range(2)]
        total = total + dot(ref[:width, :], hots[0] + hots[1])
        for k in range(2):
            gate_grads[k] = gate_grads[k] + dot(ref[width:, :], hots[k])
    for k in range(2):
        small_ref[k : k + 1, :] = column_sum(gate_grads[k][:2, :])
    product = total * normed_ref[...].astype(F32)
    small_ref[2:3, :] = column_sum(product)
    small_ref[3:, :] = jnp.zeros((5, SPAN), F32)

    @pl.when(pl.program_id(0) == 0)
    def _():
        sums_ref[...] = jnp.zeros_like(sums_ref)

    sums_ref[...] += token_sums(product)
    part = (total * inverse_ref[...] * gain_ref[...]).astype(BF)
    part_ref[...] = part
    for w_ref, out_ref in zip(w_refs, out_refs):
        out_ref[...] = dot(w_ref[...], part).astype(BF)


def collect(rows, w_pieces, slots, inverse, gain, normed):
    width, tokens = normed.shape
    blocks, parts = len(rows), len(w_pieces)
    inner = w_pieces[0].shape[0]
    return pl.pallas_call(
        lambda *refs: collect_kernel(blocks, parts, *refs),
        grid=(tokens // SPAN,),
        in_specs=[whole(*rows[0].shape)] * blocks
        + [whole(inner, width)] * parts
        + [chunked(2), chunked(1), whole(width, 1), chunked(width)],
        out_specs=[chunked(width), chunked(8), whole(8, width)] + [chunked(inner)] * parts,
        out_shape=[shape_of((width, tokens), BF), shape_of((8, tokens), F32), shape_of((8, width), F32)]
        + [shape_of((inner, tokens), BF)] * parts,
        compiler_params=WIDE,
        name="collect",
    )(*rows, *w_pieces, slots, inverse, gain, normed)


def turn_kernel(parts, me_ref, *refs):
    pieces, smalls, refs = refs[:parts], refs[parts : 2 * parts], refs[2 * parts :]
    (w_ref, gates_ref, routes_ref, normed_ref, cot_ref, inverse_ref, gain_ref, router_ref) = refs[:8]
    (do_ref, rest_ref, own_ref, router_out, sums_ref, scratch) = refs[8:]
    width, experts = router_ref.shape
    size = own_ref.shape[0]
    small = smalls[0][...]
    for ref in smalls[1:]:
        small = small + ref[...]
    grads = [small[k : k + 1, :] for k in range(2)]
    gates = [gates_ref[k : k + 1, :] for k in range(2)]
    mean = gates[0] * grads[0] + gates[1] * grads[1]
    logits = 0.0
    for k in range(2):
        hot = iota((experts, SPAN), 0) == routes_ref[k : k + 1, :]
        logits = logits + jnp.where(hot, gates[k] * (grads[k] - mean), 0.0)
    logits = logits.astype(BF)
    routed = dot(router_ref[...], logits)
    normed = normed_ref[...].astype(F32)
    product = routed * normed
    level = (small[2:3, :] + column_sum(product)) / width
    gain = gain_ref[...]
    rest = cot_ref[...].astype(F32) + inverse_ref[...] * (gain * routed - level * (normed / gain))
    scratch[...] = rest
    rest = rest.astype(BF)
    rest_ref[...] = rest
    own_ref[...] = scratch[part_rows(me_ref[0], size), :]
    do = dot(w_ref[...], rest)
    for ref in pieces:
        do = do + ref[...].astype(F32)
    do_ref[...] = do.astype(BF)

    @pl.when(pl.program_id(0) == 0)
    def _():
        router_out[...] = jnp.zeros_like(router_out)
        sums_ref[...] = jnp.zeros_like(sums_ref)

    @pl.when(me_ref[0] == 0)
    def _():
        router_out[...] += dot(logits, normed_ref[...], NT)
        sums_ref[...] += token_sums(product)


def turn(me, pieces, smalls, w, gates, routes, normed, cot, inverse, gain, router):
    width, tokens = normed.shape
    parts = len(pieces)
    inner = w.shape[0]
    experts = router.shape[1]
    return pl.pallas_call(
        lambda *refs: turn_kernel(parts, *refs),
        grid=(tokens // SPAN,),
        in_specs=[SMEM]
        + [chunked(inner)] * parts
        + [chunked(8)] * parts
        + [
            whole(inner, width), chunked(2), chunked(2), chunked(width), chunked(width),
            chunked(1), whole(width, 1), whole(width, experts),
        ],
        out_specs=[
            chunked(inner), chunked(width), chunked(width // parts), whole(experts, width), whole(8, width),
        ],
        out_shape=[
            shape_of((inner, tokens), BF),
            shape_of((width, tokens), BF),
            shape_of((width // parts, tokens), F32),
            shape_of((experts, width), F32),
            shape_of((8, width), F32),
        ],
        scratch_shapes=[pltpu.VMEM((width, SPAN), F32)],
        compiler_params=WIDE,
        name="turn",
    )(me, *pieces, *smalls, w, gates, routes, normed, cot, inverse, gain, router)


def merge_kernel(blocks, me_ref, *refs):
    row_refs, slots_ref, gates_ref = refs[:blocks], refs[blocks], refs[blocks + 1]
    outs, scratch = refs[blocks + 2 : -1], refs[-1]
    total = 0.0
    for k in range(2):
        picked = 0.0
        for b, ref in enumerate(row_refs):
            picked = picked + dot(ref[...], hot_slots(slots_ref, k, b, ref.shape[1]))
        total = total + gates_ref[k : k + 1, :] * picked
    scratch[...] = total
    for s, out in enumerate(outs):
        out[...] = scratch[part_rows(me_ref[0] ^ s, out.shape[0]), :].astype(BF)


def merge(me, rows, slots, gates, parts):
    width, tokens = rows[0].shape[0], slots.shape[1]
    return pl.pallas_call(
        lambda *refs: merge_kernel(len(rows), *refs),
        grid=(tokens // SPAN,),
        in_specs=[SMEM] + [whole(*rows[0].shape)] * len(rows) + [chunked(2), chunked(2)],
        out_specs=[chunked(width // parts)] * parts,
        out_shape=[shape_of((width // parts, tokens), BF)] * parts,
        scratch_shapes=[pltpu.VMEM((width, SPAN), F32)],
        compiler_params=WIDE,
        name="merge",
    )(me, *rows, slots, gates)


def out_weights_kernel(parts, side_ref, *refs):
    o_refs, part_ref, rest_ref, keep_ref, send_ref = refs[:parts], *refs[parts:]
    size = o_refs[0].shape[0]
    half = keep_ref.shape[1]
    for out, side in ((keep_ref, side_ref[0]), (send_ref, 1 - side_ref[0])):
        at = part_rows(side, half)
        for s, o_ref in enumerate(o_refs):
            total = dot(o_ref[...], part_ref[at, :], NT)
            if s == 0:
                total = total + dot(o_ref[...], rest_ref[at, :], NT)
            out[s * size : (s + 1) * size, :] = total.astype(BF)


def out_weights(side, o_pieces, part, rest):
    size, width = o_pieces[0].shape[0], part.shape[0]
    return pl.pallas_call(
        lambda *refs: out_weights_kernel(len(o_pieces), *refs),
        in_specs=[SMEM] + [VMEM] * (len(o_pieces) + 2),
        out_specs=[VMEM] * 2,
        out_shape=[shape_of((size * len(o_pieces), width // 2), BF)] * 2,
        compiler_params=WIDE,
        name="out_weights",
    )(side, *o_pieces, part, rest)


def leave_kernel(parts, me_ref, *refs):
    dq_ref, dk_ref, dv_ref, dkp_ref, dvp_ref, w_ref, part_ref, normed_ref, inverse_ref, gain_ref = refs[:10]
    grad_ref, small_ref, sums_ref = refs[10:13]
    outs, scratch = refs[13:-1], refs[-1]
    own = [dq_ref[...]] + [
        (a[...].astype(F32) + b[...].astype(F32)).astype(BF) for a, b in ((dk_ref, dkp_ref), (dv_ref, dvp_ref))
    ]
    grad = jnp.concatenate(own, axis=0)
    grad_ref[...] = grad
    back = dot(w_ref[...], grad)
    product = back * normed_ref[...].astype(F32)
    small_ref[...] = jnp.broadcast_to(column_sum(product), small_ref.shape)

    @pl.when(pl.program_id(0) == 0)
    def _():
        sums_ref[...] = jnp.zeros_like(sums_ref)

    sums_ref[...] += token_sums(product)
    scratch[...] = part_ref[...].astype(F32) + back * inverse_ref[...] * gain_ref[...]
    for s, out in enumerate(outs):
        out[...] = scratch[part_rows(me_ref[0] ^ s, out.shape[0]), :].astype(BF)


def leave(me, dq, dk, dv, dkp, dvp, w, part, normed, inverse, gain, parts):
    width, tokens = normed.shape
    inner = dq.shape[0]
    return pl.pallas_call(
        lambda *refs: leave_kernel(parts, *refs),
        grid=(tokens // SPAN,),
        in_specs=[SMEM]
        + [chunked(inner)] * 5
        + [whole(*w.shape), chunked(width), chunked(width), chunked(1), whole(width, 1)],
        out_specs=[chunked(3 * inner), chunked(8), whole(8, width)] + [chunked(width // parts)] * parts,
        out_shape=[shape_of((3 * inner, tokens), BF), shape_of((8, tokens), F32), shape_of((8, width), F32)]
        + [shape_of((width // parts, tokens), BF)] * parts,
        scratch_shapes=[pltpu.VMEM((width, SPAN), F32)],
        compiler_params=WIDE,
        name="leave",
    )(me, dq, dk, dv, dkp, dvp, w, part, normed, inverse, gain)


def in_weights_kernel(side_ref, normed_ref, grad_ref, keep_ref, send_ref):
    half = keep_ref.shape[0]
    keep_ref[...] = dot(normed_ref[part_rows(side_ref[0], half), :], grad_ref[...], NT).astype(BF)
    send_ref[...] = dot(normed_ref[part_rows(1 - side_ref[0], half), :], grad_ref[...], NT).astype(BF)


def in_weights(side, normed, grad):
    dims = (normed.shape[0] // 2, grad.shape[0])
    return pl.pallas_call(
        in_weights_kernel,
        in_specs=[SMEM, VMEM, VMEM],
        out_specs=[VMEM] * 2,
        out_shape=[shape_of(dims, BF)] * 2,
        compiler_params=WIDE,
        name="in_weights",
    )(side, normed, grad)


def fill_bias(near_ref, far_ref, table_ref):
    low = (iota((BUCKET, SPAN), 1) & (BUCKET - 1)) >= iota((BUCKET, SPAN), 0)
    for c in range(table_ref.shape[0] // BUCKET):
        table_ref[c * BUCKET : (c + 1) * BUCKET, :] = jnp.where(
            low, near_ref[0, c : c + 1, :], far_ref[0, c : c + 1, :]
        )


def split_bias(table_ref, count):
    table = table_ref[:count, :]
    high = table.astype(jnp.bfloat16)
    return high, (table - high.astype(jnp.float32)).astype(jnp.bfloat16)


def attend_kernel(
    cont_ref, q_ref, k_ref, v_ref, kp_ref, vp_ref, first_ref, near_ref, far_ref,
    o_ref, log_ref, table, key_own, key_prev, val_own, val_prev,
):
    count = q_ref.shape[1]
    cont = cont_ref[0] == 1
    fill_bias(near_ref, far_ref, table)
    key_own[...] = k_ref[...].T
    ones = jnp.ones((16, count), jnp.bfloat16)
    val_own[:HEAD, :] = v_ref[...]
    val_own[HEAD:, :] = ones

    def finish(o, top, cols):
        total = o[HEAD : HEAD + 1, :]
        o_ref[:, cols] = (o[:HEAD, :] / total).astype(jnp.bfloat16)
        log_ref[0, :, cols] = top + jnp.log(total)

    @pl.when(jnp.logical_not(cont))
    def _():
        for b in range(count // SPAN):
            cols = slice(b * SPAN, (b + 1) * SPAN)
            keys = (b + 1) * SPAN
            q = q_ref[:, cols] * jnp.bfloat16(HEAD**-0.5)
            s = dot(key_own[:keys, :], q) + table[count - b * SPAN : count + SPAN, :]
            s = jnp.where(iota((keys, SPAN), 0) <= iota((keys, SPAN), 1) + b * SPAN, s, NEG)
            top = jnp.max(s, axis=0, keepdims=True)
            p = jnp.exp(s - top).astype(jnp.bfloat16)
            finish(dot(val_own[:, :keys], p), top, cols)

    @pl.when(cont)
    def _():
        high, rest = split_bias(table, count)
        key_prev[:, :SPAN] = high
        key_prev[:, SPAN : 2 * SPAN] = rest
        key_prev[:, 2 * SPAN :] = kp_ref[...].T
        val_prev[:HEAD, :] = vp_ref[...]
        val_prev[HEAD:, :] = ones
        for b in range(count // SPAN):
            cols = slice(b * SPAN, (b + 1) * SPAN)
            start = max(b - 1, 0) * SPAN
            rows = slice(start, (b + 1) * SPAN)
            keys = (b + 1) * SPAN - start
            q = q_ref[:, cols] * jnp.bfloat16(HEAD**-0.5)
            first = first_ref[:, cols]
            place = iota((1, SPAN), 1) + b * SPAN
            hot = (iota((SPAN, SPAN), 0) == place - first).astype(jnp.bfloat16)
            s1 = dot(key_prev[...], jnp.concatenate([hot, hot, q], axis=0))
            s2 = dot(key_own[rows, :], q) + table[count + start - b * SPAN : count + SPAN, :]
            at = iota((keys, SPAN), 0) + start
            s2 = jnp.where((at <= place) & (at >= first), s2, NEG)
            top = jnp.maximum(
                jnp.max(s1, axis=0, keepdims=True), jnp.max(s2, axis=0, keepdims=True)
            )
            p1 = jnp.exp(s1 - top).astype(jnp.bfloat16)
            p2 = jnp.exp(s2 - top).astype(jnp.bfloat16)
            finish(dot(val_prev[...], p1) + dot(val_own[:, rows], p2), top, cols)


def attend(cont, proj, prev, first, near, far):
    heads, count = proj.shape[0] // (3 * HEAD), proj.shape[1]
    part = lambda k: pl.BlockSpec((HEAD, count), lambda h: (h + k * heads, 0))
    table = pl.BlockSpec((1,) + near.shape[1:], lambda h: (h, 0, 0))
    return pl.pallas_call(
        attend_kernel,
        grid=(heads,),
        in_specs=[
            pl.BlockSpec(memory_space=pltpu.SMEM),
            part(0), part(1), part(2), part(0), part(1),
            pl.BlockSpec((1, count), lambda h: (0, 0)),
            table, table,
        ],
        out_specs=[part(0), pl.BlockSpec((1, 1, count), lambda h: (h, 0, 0))],
        out_shape=[
            jax.ShapeDtypeStruct((heads * HEAD, count), jnp.bfloat16),
            jax.ShapeDtypeStruct((heads, 1, count), jnp.float32),
        ],
        scratch_shapes=[
            pltpu.VMEM((2 * count, SPAN), jnp.float32),
            pltpu.VMEM((count, HEAD), jnp.bfloat16),
            pltpu.VMEM((count, HEAD + 2 * SPAN), jnp.bfloat16),
            pltpu.VMEM((HEAD + 16, count), jnp.bfloat16),
            pltpu.VMEM((HEAD + 16, count), jnp.bfloat16),
        ],
        compiler_params=WIDE,
        name="attend",
    )(cont, proj, proj, proj, prev, prev, first, near, far)


def attend_back_kernel(
    cont_ref, q_ref, k_ref, v_ref, kp_ref, vp_ref, first_ref, near_ref, far_ref, o_ref, log_ref, do_ref,
    dq_ref, dk_ref, dv_ref, dkp_ref, dvp_ref, sum_near_ref, sum_far_ref,
    table, key_own, key_prev, val_own, val_prev, q_cat, q_nat, do_nat, hot_nat, dtable, dq, dk, dv,
):
    count = q_ref.shape[1]
    blocks = count // SPAN
    cont = cont_ref[0] == 1
    fill_bias(near_ref, far_ref, table)
    key_own[...] = k_ref[...].T
    val_own[...] = v_ref[...].T
    q = q_ref[...] * jnp.bfloat16(HEAD**-0.5)
    q_cat[2 * SPAN :, :] = q
    q_nat[...] = q.T
    do_nat[...] = do_ref[...].T
    dtable[...] = jnp.zeros_like(dtable)
    dq[...] = jnp.zeros_like(dq)
    dk[...] = jnp.zeros_like(dk)
    dv[...] = jnp.zeros_like(dv)
    delta = jnp.sum(
        do_ref[...].astype(jnp.float32) * o_ref[...].astype(jnp.float32), axis=0, keepdims=True
    )

    def tile(kb, qb):
        rows = slice(kb * SPAN, (kb + 1) * SPAN)
        cols = slice(qb * SPAN, (qb + 1) * SPAN)
        where = slice(count + (kb - qb) * SPAN, count + (kb - qb + 1) * SPAN)
        s = dot(key_own[rows, :], q_cat[2 * SPAN :, cols]) + table[where, :]
        at = iota((SPAN, SPAN), 0) + kb * SPAN
        live = (at <= iota((SPAN, SPAN), 1) + qb * SPAN) & (at >= first_ref[:, cols])
        p = jnp.exp(jnp.where(live, s, NEG) - log_ref[0, :, cols])
        dp = dot(val_own[rows, :], do_ref[:, cols])
        ds = p * (dp - delta[:, cols])
        dtable[where, :] += ds
        ds = ds.astype(jnp.bfloat16)
        dk[rows, :] += dot(ds, q_nat[cols, :])
        dv[rows, :] += dot(p.astype(jnp.bfloat16), do_nat[cols, :])
        dq[:, cols] += dot(k_ref[:, rows], ds)

    for kb in range(blocks):
        for qb in range(kb, min(kb + 2, blocks)):
            tile(kb, qb)

    @pl.when(jnp.logical_not(cont))
    def _():
        for kb in range(blocks):
            for qb in range(kb + 2, blocks):
                tile(kb, qb)

    @pl.when(cont)
    def _():
        high, rest = split_bias(table, count)
        key_prev[:, :SPAN] = high
        key_prev[:, SPAN : 2 * SPAN] = rest
        key_prev[:, 2 * SPAN :] = kp_ref[...].T
        val_prev[...] = vp_ref[...].T
        hot = (iota((SPAN, count), 0) == iota((1, count), 1) - first_ref[...]).astype(jnp.bfloat16)
        q_cat[:SPAN, :] = hot
        q_cat[SPAN : 2 * SPAN, :] = hot
        hot_nat[...] = hot.T

        for kb in range(blocks):
            rows = slice(kb * SPAN, (kb + 1) * SPAN)
            s = dot(key_prev[rows, :], q_cat[...])
            p = jnp.exp(s - log_ref[0])
            dp = dot(val_prev[rows, :], do_ref[...])
            ds = (p * (dp - delta)).astype(jnp.bfloat16)
            dkp_ref[:, rows] = dot(ds, q_nat[...]).astype(jnp.bfloat16).T
            dvp_ref[:, rows] = dot(p.astype(jnp.bfloat16), do_nat[...]).astype(jnp.bfloat16).T
            dtable[rows, :] += dot(ds, hot_nat[...])
            dq[...] += dot(kp_ref[:, rows], ds)

    dq_ref[...] = (dq[...] * HEAD**-0.5).astype(jnp.bfloat16)
    dk_ref[...] = dk[...].astype(jnp.bfloat16).T
    dv_ref[...] = dv[...].astype(jnp.bfloat16).T
    low = (iota((BUCKET, SPAN), 1) & (BUCKET - 1)) >= iota((BUCKET, SPAN), 0)
    for c in range(2 * count // BUCKET):
        part = dtable[c * BUCKET : (c + 1) * BUCKET, :]
        near = jnp.sum(jnp.where(low, part, 0.0), axis=0, keepdims=True)
        sum_near_ref[0, c : c + 1, :] = near
        sum_far_ref[0, c : c + 1, :] = jnp.sum(part, axis=0, keepdims=True) - near


def attend_back(cont, proj, prev, first, near, far, o, log, do):
    heads, count = proj.shape[0] // (3 * HEAD), proj.shape[1]
    part = lambda k: pl.BlockSpec((HEAD, count), lambda h: (h + k * heads, 0))
    table = pl.BlockSpec((1,) + near.shape[1:], lambda h: (h, 0, 0))
    grad = jax.ShapeDtypeStruct((heads * HEAD, count), jnp.bfloat16)
    sums = jax.ShapeDtypeStruct(near.shape, jnp.float32)
    return pl.pallas_call(
        attend_back_kernel,
        grid=(heads,),
        in_specs=[
            pl.BlockSpec(memory_space=pltpu.SMEM),
            part(0), part(1), part(2), part(0), part(1),
            pl.BlockSpec((1, count), lambda h: (0, 0)),
            table, table, part(0),
            pl.BlockSpec((1, 1, count), lambda h: (h, 0, 0)),
            part(0),
        ],
        out_specs=[part(0)] * 5 + [table] * 2,
        out_shape=[grad] * 5 + [sums] * 2,
        scratch_shapes=[
            pltpu.VMEM((2 * count, SPAN), jnp.float32),
            pltpu.VMEM((count, HEAD), jnp.bfloat16),
            pltpu.VMEM((count, HEAD + 2 * SPAN), jnp.bfloat16),
            pltpu.VMEM((count, HEAD), jnp.bfloat16),
            pltpu.VMEM((count, HEAD), jnp.bfloat16),
            pltpu.VMEM((HEAD + 2 * SPAN, count), jnp.bfloat16),
            pltpu.VMEM((count, HEAD), jnp.bfloat16),
            pltpu.VMEM((count, HEAD), jnp.bfloat16),
            pltpu.VMEM((count, SPAN), jnp.bfloat16),
            pltpu.VMEM((2 * count, SPAN), jnp.float32),
            pltpu.VMEM((HEAD, count), jnp.float32),
            pltpu.VMEM((count, HEAD), jnp.float32),
            pltpu.VMEM((count, HEAD), jnp.float32),
        ],
        compiler_params=WIDE,
        name="attend_back",
    )(cont, proj, proj, proj, prev, prev, first, near, far, o, log, do)


def bias_levels(bias, count):
    rows, lanes = 2 * count // BUCKET, SPAN // BUCKET
    step = jnp.arange(lanes)[None, :] - jnp.arange(rows)[:, None] + rows // 2
    names = jnp.arange(NB)
    near_hot = (jnp.clip(step, 0, NB - 1)[..., None] == names).astype(jnp.float32)
    far_hot = (jnp.clip(step - 1, 0, NB - 1)[..., None] == names).astype(jnp.float32)
    return near_hot, far_hot


def bias_tables(bias, count):
    out = []
    for hot in bias_levels(bias, count):
        level = jnp.sum(hot[None] * bias[:, None, None, :], axis=-1)
        out.append(jnp.repeat(level, BUCKET, axis=2))
    return out


def bias_totals(sum_near, sum_far, count):
    total = 0.0
    for hot, sums in zip(bias_levels(None, count), (sum_near, sum_far)):
        level = jnp.sum(sums.reshape(sums.shape[0], sums.shape[1], -1, BUCKET), axis=-1)
        total = total + jnp.sum(level[..., None] * hot[None], axis=(1, 2))
    return total


def body(
    block_entry_rows,
    cotangent,
    gain_one,
    w_qkv,
    w_out_attn,
    rel_bias,
    gain_two,
    router,
    w_in,
    w_out,
    routes,
    slot_order,
    cont_ids,
):
    tokens, feats = block_entry_rows.shape
    width, experts = router.shape
    per_dev = w_in.shape[0]
    owners = experts // per_dev
    cap = 2 * tokens // experts
    inner = w_qkv.shape[2]
    heads = inner // HEAD
    parts = lax.axis_size("mx")
    my_part, my_owner, my_side = lax.axis_index("mx"), lax.axis_index("dp"), lax.axis_index("my")
    me, side = my_part.astype(jnp.int32).reshape(1), my_side.astype(jnp.int32).reshape(1)
    is_cont = my_side == 1
    by_owner = cap % 128 == 0
    count, block = (owners, cap) if by_owner else (1, owners * cap)

    def trade(rows):
        if by_owner:
            return exchange(rows, "dp")
        return [lax.all_to_all(rows[0], "dp", split_axis=1, concat_axis=1, tiled=True)]

    x_own, c_own = block_entry_rows.T, cotangent.T
    x_pieces = spread(x_own, "mx")
    qkv_full = lax.all_gather(w_qkv, "my", axis=0, tiled=True).reshape(width, 3 * inner)
    out_own = lax.all_gather(w_out_attn, "my", axis=1, tiled=True)
    win_full = lax.all_gather(w_in, "my", axis=1, tiled=True)
    wout_full = lax.all_gather(w_out, "my", axis=2, tiled=True)
    gain_a, gain_b = gain_one[:, None], gain_two[:, None]

    ids = jnp.arange(experts)
    owner = ids // per_dev
    owner = owner ^ my_owner if by_owner else owner
    base = (((ids % per_dev) * owners + owner) * cap).astype(F32)[:, None]
    routes = routes.T
    slots = slot_rows(base, routes, slot_order, cap)

    index = jnp.arange(tokens, dtype=jnp.int32)
    same_seg = cont_ids[0][:, None] == cont_ids[0][None, :]
    first = jnp.min(jnp.where(same_seg, index[:, None], tokens), axis=0, keepdims=True)
    first = jnp.where(is_cont, first, 0)
    bias_own = lax.dynamic_slice_in_dim(rel_bias, my_part * heads, heads, 0)
    near, far = bias_tables(bias_own, tokens)

    x_full, normed_one, proj, inverse_one = project(me, x_pieces, qkv_full, gain_a)
    earlier = lax.ppermute(proj[inner:], "my", [(0, 1)])
    geometry = (side, proj, earlier, first, near, far)
    o_own, logs = attend(*geometry)
    o_pieces = spread(o_own, "mx")
    out_pieces = spread(out_own, "mx")
    c_pieces = spread(c_own, "mx")
    c_full, *c_rows = send_rows(me, c_pieces, slots, per_dev * count, block)
    c_rows = [trade(c_rows[j * count : (j + 1) * count]) for j in range(per_dev)]
    h_own, inverse_two, normed_two, gates, *rows = enter(
        me, o_pieces, out_pieces, x_full, gain_b, router, routes, slots, per_dev * count, block
    )
    rows = [trade(rows[j * count : (j + 1) * count]) for j in range(per_dev)]

    back_rows, kept = [], []
    for j in range(per_dev):
        *back, act, pre, sent = expert(rows[j], c_rows[j], win_full[j], wout_full[j])
        back_rows += trade(back)
        kept.append((act, pre, sent))
    part, small, gain_b_sums, *do_blocks = collect(
        back_rows, out_pieces, slots, inverse_two, gain_b, normed_two
    )
    do_pieces = exchange(do_blocks, "mx")
    smalls = spread(small, "mx")
    do, rest, rest_own, router_sums, gain_b_rest = turn(
        me, do_pieces, smalls, out_own, gates, routes, normed_two, c_full, inverse_two, gain_b, router
    )

    expert_rows, win_grads, wout_grads = [], [], []
    for j, (act, pre, sent) in enumerate(kept):
        expert_rows += trade(expert_out(act, wout_full[j], count))
        in_keep, in_send, out_keep, out_send = expert_weights(side, rows[j], act, pre, sent)
        win_grads.append(in_keep + swap(in_send, "my", 1).astype(F32))
        wout_grads.append(out_keep + swap(out_send, "my", 1).astype(F32))
    mixed = exchange(merge(me, expert_rows, slots, gates, parts), "mx")
    block_output = h_own
    for piece in mixed:
        block_output = block_output + piece.astype(F32)

    dq, dk, dv, dkp, dvp, near_sums, far_sums = attend_back(*geometry, o_own, logs, do)
    dkp, dvp = lax.ppermute((dkp, dvp), "my", [(1, 0)])
    grad, small, gain_a_sums, *x_blocks = leave(
        me, dq, dk, dv, dkp, dvp, qkv_full, part, normed_one, inverse_one, gain_a, parts
    )
    x_blocks = exchange(x_blocks, "mx")
    level = sum(piece[:1] for piece in spread(small, "mx")) / width
    d_x = rest_own - level * inverse_one * inverse_one * x_own.astype(F32)
    for piece in x_blocks:
        d_x = d_x + piece.astype(F32)

    keep, send = out_weights(side, o_pieces, part, rest)
    keep = (keep.astype(F32) + swap(send, "my", 1).astype(F32)).astype(BF)
    keep = exchange([keep[s * inner : (s + 1) * inner] for s in range(parts)], "mx")
    d_w_out_attn = cube_sum(sum(piece.astype(F32) for piece in keep), "dp", BF)
    keep, send = in_weights(side, normed_one, grad)
    d_w_qkv = cube_sum(keep.astype(F32) + swap(send, "my", 1).astype(F32), "dp", BF)

    bias_grad = lax.dynamic_update_slice_in_dim(
        jnp.zeros(rel_bias.shape, F32), bias_totals(near_sums, far_sums, tokens), my_part * heads, 0
    ).reshape(1, -1)
    bias_grad = jnp.pad(bias_grad, ((0, 0), (0, width - bias_grad.shape[1])))
    sums = jnp.concatenate([gain_a_sums[:1], gain_b_sums[:1] + gain_b_rest[:1], bias_grad, router_sums], axis=0)
    for axis in ("my", "dp", "mx"):
        sums = cube_sum(sums, axis, F32)
    return (
        block_output.T,
        d_x.T,
        d_w_qkv.reshape(width // 2, 3, inner),
        d_w_out_attn,
        sums[2, : rel_bias.size].reshape(rel_bias.shape),
        sums[0] / gain_one,
        sums[1] / gain_two,
        sums[3:].T,
        jnp.stack(win_grads),
        jnp.stack(wout_grads),
    )


def solution(mesh):
    return jax.shard_map(
        body,
        mesh=mesh,
        in_specs=(
            P(("dp", "my"), "mx"),
            P(("dp", "my"), "mx"),
            P(),
            P("my", None, "mx"),
            P("mx", "my"),
            P(),
            P(),
            P(),
            P("dp", "my", "mx"),
            P("dp", "mx", "my"),
            P(("dp", "my"), None),
            P(("dp", "my"), None),
            P("dp", None),
        ),
        out_specs=(
            P(("dp", "my"), "mx"),
            P(("dp", "my"), "mx"),
            P("my", None, "mx"),
            P("mx", "my"),
            P(),
            P(),
            P(),
            P(),
            P("dp", "my", "mx"),
            P("dp", "mx", "my"),
        ),
        check_vma=False,
    )
```
